256 devices in a mesh: dp: 32 (over z_lo, x, core), rows: 8 (over z_hi, y).
Axes of the slice: x: 4, y: 4, z: 8 (z_hi: 2, z_lo: 4; z = z_hi * 4 + z_lo), core: 2. Of those that a mesh axis runs over, the one named last changes fastest.
Arguments:
- features: bfloat16 [64, 48, 64, 1024], P('dp', 'rows'), may hold values from -8 to 8
- first_atrous_weight: bfloat16 [3, 3, 1024, 256], P(None, None, 'dp'), may hold values from -0.0625 to 0.0625
- second_atrous_weight: bfloat16 [3, 3, 1024, 256], P(None, None, 'dp'), may hold values from -0.0625 to 0.0625
- third_atrous_weight: bfloat16 [3, 3, 1024, 256], P(None, None, 'dp'), may hold values from -0.0625 to 0.0625
- pointwise_weight: bfloat16 [1024, 256], replicated, may hold values from -0.1875 to 0.1875
- pooling_weight: bfloat16 [1024, 256], replicated, may hold values from -0.1875 to 0.1875
- projection_weight: bfloat16 [1280, 256], replicated, may hold values from -0.15625 to 0.15625
- branch_norm_gain: float32 [4, 256], replicated, may hold values from 0.25 to 1.75
- branch_norm_shift: float32 [4, 256], replicated, may hold values from -3 to 3
- projection_norm_gain: float32 [256], replicated, may hold values from 0.25 to 1.75
- projection_norm_shift: float32 [256], replicated, may hold values from -3 to 3
- ghost_group_index: int32 [64], replicated, may hold values from 0 to 15, as said below
Outputs:
- decoder_in: bfloat16 [64, 48, 64, 256], P(None, 'rows', 'dp')
The draws below stay inside these ranges and needn't reach their ends.
Inputs may be any that keep to these rules, and one draw needn't show every extreme that they name: `ghost_group_index`: each of the 16 group ids names exactly 4 images.
All inputs are finite; a program needn't handle non-finite values.
Results may differ from the reference program's by a relative error of at most 0.0014.
The reference program's roundings to bfloat16 on the way (of `branches`, `pooled`, `pool_act` and `joined`) count: a program that leaves them out, or rounds other values in their place, can miss the bound.
Values may be sent and summed in bfloat16 or wider, within the bound.
A program may use at most 128 MiB of HBM per device.

```python
import jax
import jax.numpy as jnp
from jax import lax

INPUT_CHANNELS = 1024
OUTPUT_CHANNELS = 256
COLS = 64
DILATION_FIRST = 12
DILATION_SECOND = 24
DILATION_THIRD = 36
IMAGES = 64
MAP_ROWS = 48
GROUPS = 16


def draw_features(key, part):
    first_key = jax.random.fold_in(key, 11)
    second_key = jax.random.fold_in(key, 12)
    base = jax.random.normal(first_key, (IMAGES, MAP_ROWS, COLS, INPUT_CHANNELS), jnp.float32)
    offset = jax.random.normal(second_key, (IMAGES, 1, 1, INPUT_CHANNELS), jnp.float32)
    return jnp.clip(base + offset, -8.0, 8.0).astype(jnp.bfloat16)


def draw_ghost_group_index(key, part):
    order = jax.random.permutation(jax.random.fold_in(key, 21), IMAGES)
    return (order // 4).astype(jnp.int32)


def level_of(own_key, dims, pieces, smallest, top_value):
    level, own = 1.0, jax.random.fold_in(own_key, 6)
    for position, parts in pieces:
        heights = jnp.exp(jax.random.uniform(jax.random.fold_in(own, position), (parts,), jnp.float32, smallest / len(pieces), top_value / len(pieces)))
        level = level * jnp.repeat(heights, dims[position] // parts).reshape([-1 if axis == position else 1 for axis in range(len(dims))])
    return level


def bell_draw(key, shape, spread, most, split=(), kind=jnp.bfloat16):
    level = level_of(key, shape, split, -0.22, 0.18) if split else 1.0
    result = jax.random.normal(key, shape, jnp.float32) * spread * level
    return jnp.minimum(jnp.maximum(result, -most), most).astype(kind)


def setup_inputs(seed: int = 0) -> dict:
    key_of = jax.random.split(jax.random.key(seed), 13)
    return {
        "features": draw_features(jax.random.fold_in(key_of[12], 71), 0),
        "first_atrous_weight": bell_draw(key_of[1], (3, 3, INPUT_CHANNELS, OUTPUT_CHANNELS), (9 * INPUT_CHANNELS) ** -0.5, 0.0625, ((2, 32),)),
        "second_atrous_weight": bell_draw(key_of[2], (3, 3, INPUT_CHANNELS, OUTPUT_CHANNELS), (9 * INPUT_CHANNELS) ** -0.5, 0.0625, ((2, 32),)),
        "third_atrous_weight": bell_draw(key_of[3], (3, 3, INPUT_CHANNELS, OUTPUT_CHANNELS), (9 * INPUT_CHANNELS) ** -0.5, 0.0625, ((2, 32),)),
        "pointwise_weight": bell_draw(key_of[4], (INPUT_CHANNELS, OUTPUT_CHANNELS), INPUT_CHANNELS ** -0.5, 0.1875),
        "pooling_weight": bell_draw(key_of[5], (INPUT_CHANNELS, OUTPUT_CHANNELS), INPUT_CHANNELS ** -0.5, 0.1875),
        "projection_weight": bell_draw(key_of[6], (5 * OUTPUT_CHANNELS, OUTPUT_CHANNELS), (5 * OUTPUT_CHANNELS) ** -0.5, 0.15625),
        "branch_norm_gain": jnp.clip(1.0 + 0.15 * jax.random.normal(key_of[7], (4, OUTPUT_CHANNELS), jnp.float32), 0.25, 1.75),
        "branch_norm_shift": bell_draw(key_of[8], (4, OUTPUT_CHANNELS), 0.5, 3.0, (), jnp.float32),
        "projection_norm_gain": jnp.clip(1.0 + 0.15 * jax.random.normal(key_of[9], (OUTPUT_CHANNELS,), jnp.float32), 0.25, 1.75),
        "projection_norm_shift": bell_draw(key_of[10], (OUTPUT_CHANNELS,), 0.5, 3.0, (), jnp.float32),
        "ghost_group_index": draw_ghost_group_index(jax.random.fold_in(key_of[12], 71), 0),
    }


def atrous_branch(image_slice, kernel_weight, dilation_rate):
    branch_output = lax.conv_general_dilated(image_slice[None], kernel_weight, (1, 1), [(dilation_rate, dilation_rate), (dilation_rate, dilation_rate)], rhs_dilation=(dilation_rate, dilation_rate), dimension_numbers=('NHWC', 'HWIO', 'NHWC'), preferred_element_type=jnp.float32)
    return branch_output[0]

def ghost_norm(pre, onehot, gain, shift):
    count = 4.0 * MAP_ROWS * COLS
    first = lax.optimization_barrier(jnp.sum(pre, axis=(1, 2)))
    second = lax.optimization_barrier(jnp.sum(pre * pre, axis=(1, 2)))
    mean = jnp.dot(onehot.T, first, precision=lax.Precision.HIGHEST) / count
    var = jnp.dot(onehot.T, second, precision=lax.Precision.HIGHEST) / count - mean * mean
    inv = lax.rsqrt(var + 1e-05)
    img_mean = jnp.dot(onehot, mean, precision=lax.Precision.HIGHEST)
    img_inv = jnp.dot(onehot, inv, precision=lax.Precision.HIGHEST)
    scaled = (pre - img_mean[:, None, None, :]) * img_inv[:, None, None, :] * gain + shift
    return jax.nn.relu(scaled).astype(jnp.bfloat16)

def reference(features, first_atrous_weight, second_atrous_weight, third_atrous_weight, pointwise_weight, pooling_weight, projection_weight, branch_norm_gain, branch_norm_shift, projection_norm_gain, projection_norm_shift, ghost_group_index):
    onehot = (ghost_group_index[:, None] == jnp.arange(GROUPS, dtype=jnp.int32)[None, :]).astype(jnp.float32)

    def per_image(image_slice):
        pointwise_output = jnp.einsum('hwc,co->hwo', image_slice, pointwise_weight, preferred_element_type=jnp.float32)
        return jnp.concatenate([pointwise_output, atrous_branch(image_slice, first_atrous_weight, DILATION_FIRST), atrous_branch(image_slice, second_atrous_weight, DILATION_SECOND), atrous_branch(image_slice, third_atrous_weight, DILATION_THIRD)], -1)
    pre = lax.map(per_image, features)
    branches = ghost_norm(pre, onehot, branch_norm_gain.reshape(-1), branch_norm_shift.reshape(-1))
    pooled = (lax.optimization_barrier(jnp.sum(features, axis=(1, 2), dtype=jnp.float32)) / (MAP_ROWS * COLS)).astype(jnp.bfloat16)
    pool_act = jax.nn.relu(jnp.dot(pooled, pooling_weight, preferred_element_type=jnp.float32)).astype(jnp.bfloat16)
    pool_map = jnp.broadcast_to(pool_act[:, None, None, :], (IMAGES, MAP_ROWS, COLS, OUTPUT_CHANNELS))
    joined = jnp.concatenate([branches, pool_map], -1)
    proj = jnp.einsum('nhwc,co->nhwo', joined, projection_weight, preferred_element_type=jnp.float32)
    return ghost_norm(proj, onehot, projection_norm_gain, projection_norm_shift)
```

```python
import functools

import jax
import jax.numpy as jnp
from jax import lax
from jax.experimental import pallas as pl
from jax.experimental.pallas import tpu as pltpu
from jax.sharding import PartitionSpec as P

MESH = pl.DeviceIdType.MESH
F32 = jnp.float32
BF16 = jnp.bfloat16
ORDER = ((0, 1), (1, 1), (2, 1), (0, 0), (0, 2), (1, 0), (1, 2), (2, 0), (2, 2))
CHUNKS = len(ORDER)
COUNT = 4.0 * 48 * 64
PIXELS = 48.0 * 64


def device(x, y, z, c):
    x, y, z, c = lax.rem(x + 4, 4), lax.rem(y + 4, 4), lax.rem(z + 8, 8), lax.rem(c, 2)
    return (lax.rem(z, 4) * 8 + x * 2 + c, (z // 4) * 4 + y)


def remote(src, dst, send, recv, to):
    return pltpu.make_async_remote_copy(
        src_ref=src, dst_ref=dst, send_sem=send, recv_sem=recv, device_id=to, device_id_type=MESH
    )


def kernel(
    feat, wa, wb, wc, point_w, pool_w, proj_w, gain, shift, pgain, pshift, group,
    out,
    wbuf, xbuf, xright, xleft, acc, proj, rows, tiles, sendbuf, pool_buf,
    msg_a, got_a, red_a, sum_y_a, sum_z_a, all_a,
    msg_b, got_b, red_b, sum_y_b, sum_z_b, all_b,
    local_sem, ws, wr, fs, fr, ps, pr, as_a, ar_a, as_b, ar_b, end_send, end_recv,
):
    d, r = lax.axis_index("dp"), lax.axis_index("rows")
    z_lo, x, c = d // 8, lax.rem(d // 2, 4), lax.rem(d, 2)
    z_hi, y = r // 4, lax.rem(r, 4)
    z = z_hi * 4 + z_lo
    parity, half = lax.rem(y, 2), y // 2
    own = z_hi * 2 + half
    image = (d // 2) * 4 + own
    other = 1 - c
    y_pair = y + 1 - 2 * parity
    up, down = device(x, y, z + 1, c), device(x, y, z - 1, c)
    right, left = device(x + 1, y, z, c), device(x - 1, y, z, c)
    sibling = device(x, y, z, other)
    pool_peers = (sibling, device(x, y_pair, z, c), device(x, y_pair, z, other))

    locals_ = [
        pltpu.make_async_copy(w, wbuf.at[pl.ds(9 * i, 9), z_lo, x, c], local_sem.at[i])
        for i, w in enumerate((wa, wb, wc))
    ]
    for cp in locals_:
        cp.start()

    barrier = pltpu.get_barrier_semaphore()
    for peer in (up, down, right, left) + pool_peers:
        pl.semaphore_signal(barrier, inc=1, device_id=peer, device_id_type=MESH)
    for b in range(4):
        src = device(x, 2 * (b % 2) + parity, (b // 2) * 4 + z_lo, z_hi)

        @pl.when(jnp.logical_not(jnp.logical_and(own == b, c == z_hi)))
        def _():
            pl.semaphore_signal(barrier, inc=1, device_id=src, device_id_type=MESH)

    @pl.when(c == z_hi)
    def _():
        pl.semaphore_wait(barrier, 10)

    @pl.when(c != z_hi)
    def _():
        pl.semaphore_wait(barrier, 11)

    for cp in locals_:
        cp.wait()

    def taps(k):
        b, kh = ORDER[k]
        return pl.ds(9 * b + 3 * kh, 3)

    def shard(k, zz, rows=None):
        ref = wbuf.at[taps(k), zz, x, c]
        return ref if rows is None else wbuf.at[taps(k), zz, x, c, pl.ds(rows, 16)]

    def column(k, xx, cc, zs=None):
        return wbuf.at[taps(k), slice(None) if zs is None else pl.ds(zs, 2), xx, cc]

    z_next, z_prev = lax.rem(z_lo + 1, 4), lax.rem(z_lo + 3, 4)
    z_far = lax.rem(z_lo + 2, 4)
    x_next, x_prev, x_far = lax.rem(x + 1, 4), lax.rem(x + 3, 4), lax.rem(x + 2, 4)

    def to(ref, k, i, peer):
        return remote(ref, ref, ws.at[k, i], wr.at[k, i], peer)

    sent = []

    def send(ref, k, i, peer):
        cp = to(ref, k, i, peer)
        cp.start()
        sent.append(cp)

    def arrived(ref, k, i):
        to(ref, k, i, sibling).wait_recv()

    for k in range(2):
        send(shard(k, z_lo), k, 0, up)
        send(shard(k, z_lo), k, 1, down)

    for i in range(2):
        for h in range(2):
            src = feat.at[i, pl.ds(3 * h, 3)]
            is_self = jnp.logical_and(jnp.logical_and(c == z_hi, c == h), half == i)

            @pl.when(is_self)
            def _():
                pltpu.make_async_copy(src, xbuf.at[own], fr.at[own]).start()

            @pl.when(jnp.logical_not(is_self))
            def _():
                remote(
                    src, xbuf.at[own], fs.at[2 * i + h], fr.at[own],
                    device(x, 2 * i + parity, c * 4 + z_lo, jnp.int32(h)),
                ).start()

    for k in range(2, CHUNKS):
        send(shard(k, z_lo), k, 0, up)
        send(shard(k, z_lo), k, 1, down)

    def features_arrive():
        for b in range(4):
            pltpu.make_async_copy(xbuf.at[b], xbuf.at[b], fr.at[b]).wait()
        part = jnp.zeros((8, 1024), F32)
        col = lax.broadcasted_iota(jnp.int32, (64, 1024), 0)

        def body(t, part):
            v = xbuf[t // 3, lax.rem(t, 3)].astype(F32)
            xright[t // 3, lax.rem(t, 3)] = jnp.where(col >= 4, pltpu.roll(v, 4, 0), 0.0).astype(BF16)
            xleft[t // 3, lax.rem(t, 3)] = jnp.where(col < 60, pltpu.roll(v, 60, 0), 0.0).astype(BF16)
            return part + v.reshape(8, 8, 1024).sum(axis=0)

        pool_buf[0] = lax.fori_loop(0, 12, body, part)
        for i, peer in enumerate(pool_peers):
            remote(pool_buf.at[0], pool_buf.at[i + 1], ps.at[i], pr.at[i], peer).start()

        def point(b, _):
            acc[b, :, :, 0:256] = jnp.dot(
                xbuf[b].reshape(192, 1024), point_w[...], preferred_element_type=F32
            ).reshape(3, 64, 256)
            return 0

        lax.fori_loop(0, 4, point, 0)

    def compute(k):
        branch, kh = ORDER[k]
        step = branch + 1
        x0 = (0, 0, step)[kh]
        o0 = (step, 0, 0)[kh]
        blocks = 4 if kh == 1 else 4 - step
        lanes = slice(256 * (branch + 1), 256 * (branch + 2))

        def body(t, _):
            b, o = x0 + t, o0 + t

            def times(lhs, kw):
                n = lhs.shape[1]
                w = wbuf[9 * branch + 3 * kh + kw].reshape(1024, 256)
                return jnp.dot(
                    lhs.reshape(3 * n, 1024), w, preferred_element_type=F32
                ).reshape(3, n, 256)

            mid = times(xbuf[b], 1)
            if kh == 1:
                acc[o, :, :, lanes] = mid
            else:
                acc[o, :, :, lanes] += mid
            if branch == 0:
                acc[o, :, 8:64, lanes] += times(xright[b], 0)[:, 0:56]
                acc[o, :, 0:56, lanes] += times(xleft[b], 2)[:, 8:64]
            elif branch == 1:
                acc[o, :, 24:64, lanes] += times(xbuf[b, :, 0:48], 0)[:, 0:40]
                acc[o, :, 0:40, lanes] += times(xbuf[b, :, 16:64], 2)[:, 8:48]
            else:
                acc[o, :, 32:64, lanes] += times(xright[b, :, 0:32], 0)
                acc[o, :, 0:32, lanes] += times(xleft[b, :, 32:64], 2)
            return 0

        lax.fori_loop(0, blocks, body, 0)

    for t in range(CHUNKS + 4):
        k = t
        if 0 <= k < CHUNKS:
            arrived(shard(k, z_prev), k, 0)
            send(shard(k, z_prev, 16), k, 2, up)
            arrived(shard(k, z_next), k, 1)
            send(shard(k, z_next, 0), k, 3, down)
        k = t - 1
        if 0 <= k < CHUNKS:
            arrived(shard(k, z_far, 16), k, 2)
            arrived(shard(k, z_far, 0), k, 3)
            send(column(k, x, c), k, 4, right)
            send(column(k, x, c), k, 5, left)
            send(column(k, x, c), k, 8, sibling)
        k = t - 2
        if 0 <= k < CHUNKS:
            arrived(column(k, x_prev, c), k, 4)
            send(column(k, x_prev, c, 2), k, 6, right)
            arrived(column(k, x_next, c), k, 5)
            send(column(k, x_next, c, 0), k, 7, left)
            send(column(k, x_prev, c), k, 9, sibling)
            send(column(k, x_next, c), k, 10, sibling)
        k = t - 3
        if 0 <= k < CHUNKS:
            arrived(column(k, x_far, c, 2), k, 6)
            arrived(column(k, x_far, c, 0), k, 7)
            send(column(k, x_far, c), k, 11, sibling)
        if t == 7:
            features_arrive()
        for k in (2 * (t - 8), 2 * (t - 8) + 1):
            if 0 <= k < CHUNKS:
                arrived(column(k, x, other), k, 8)
                arrived(column(k, x_prev, other), k, 9)
                arrived(column(k, x_next, other), k, 10)
                arrived(column(k, x_far, other), k, 11)
                compute(k)

    for cp in sent:
        cp.wait_send()

    mine = group[image]
    spot = x * 2 + c

    def all_reduce(msg, got, red, sum_y, sum_z, full, s_sem, r_sem):
        def peer(o):
            s = lax.rem(spot + o, 8)
            return s, device(s // 2, y, z, lax.rem(s, 2))

        copies = []

        def go(src, dst, i, to_):
            cp = remote(src, dst, s_sem.at[i], r_sem.at[i], to_)
            cp.start()
            copies.append(cp)

        for o in range(1, 8):
            s, to_ = peer(o)
            go(msg.at[s], got.at[o - 1], o - 1, to_)
        total = msg[spot]
        for o in range(1, 8):
            copies[o - 1].wait_recv()
            total = total + got[o - 1]
        red[0] = total
        for o in range(1, 4):
            go(red.at[0], sum_y.at[o - 1], 6 + o, device(x, y + o, z, c))
        for o in range(1, 4):
            copies[6 + o].wait_recv()
            total = total + sum_y[o - 1]
        red[1] = total
        for o in range(1, 8):
            go(red.at[1], sum_z.at[o - 1], 9 + o, device(x, y, z + o, c))
        for o in range(1, 8):
            copies[9 + o].wait_recv()
            total = total + sum_z[o - 1]
        full[spot] = total
        for o in range(1, 8):
            s, to_ = peer(o)
            go(full.at[spot], full.at[spot], 16 + o, to_)
        for o in range(1, 8):
            s = lax.rem(spot - o + 8, 8)
            remote(full.at[s], full.at[s], s_sem.at[16 + o], r_sem.at[16 + o], sibling).wait_recv()
        return copies

    def add_up(t, carry):
        first, second = carry
        v = acc[t // 3, lax.rem(t, 3)].reshape(8, 8, 1024)
        return first + v.sum(axis=0), second + (v * v).sum(axis=0)

    zero = jnp.zeros((8, 1024), F32)
    first, second = lax.fori_loop(0, 12, add_up, (zero, zero))
    first = jnp.sum(first, axis=0, keepdims=True)
    second = jnp.sum(second, axis=0, keepdims=True)
    labels = lax.broadcasted_iota(jnp.int32, (16, 128), 0)
    for s in range(8):
        lanes = slice(128 * s, 128 * (s + 1))
        msg_a[s, 0:16] = jnp.where(labels == mine, first[:, lanes], 0.0)
        msg_a[s, 16:32] = jnp.where(labels == mine, second[:, lanes], 0.0)
    waits = all_reduce(msg_a, got_a, red_a, sum_y_a, sum_z_a, all_a, as_a, ar_a)

    means, invs = [], []
    for s in range(8):
        g1 = jnp.sum(jnp.where(labels == mine, all_a[s, 0:16], 0.0), axis=0, keepdims=True)
        g2 = jnp.sum(jnp.where(labels == mine, all_a[s, 16:32], 0.0), axis=0, keepdims=True)
        mean = g1 / COUNT
        means.append(mean)
        invs.append(lax.rsqrt(g2 / COUNT - mean * mean + 1e-05))
    mean = jnp.concatenate(means, axis=1)
    inv = jnp.concatenate(invs, axis=1)

    for i in range(3):
        remote(pool_buf.at[i + 1], pool_buf.at[i + 1], ps.at[i], pr.at[i], sibling).wait()
    pool = pool_buf[0] + pool_buf[1] + pool_buf[2] + pool_buf[3]
    pooled = (jnp.sum(pool, axis=0, keepdims=True) / PIXELS).astype(BF16)
    pooled = jnp.broadcast_to(pooled, (16, 1024))
    act = jnp.maximum(jnp.dot(pooled, pool_w[...], preferred_element_type=F32), 0.0).astype(BF16)
    pool_row = jnp.dot(act, proj_w[1024:1280], preferred_element_type=F32)[0:1]

    def project(b, carry):
        first, second = carry
        v = acc[b].reshape(192, 1024)
        v = (v - mean) * inv * gain[...] + shift[...]
        v = jnp.maximum(v, 0.0).astype(BF16)
        p = jnp.dot(v, proj_w[0:1024], preferred_element_type=F32) + pool_row
        proj[b] = p
        p = p.reshape(24, 8, 256)
        return first + p.sum(axis=0), second + (p * p).sum(axis=0)

    zero = jnp.zeros((8, 256), F32)
    first, second = lax.fori_loop(0, 4, project, (zero, zero))
    first = jnp.sum(first, axis=0, keepdims=True)
    second = jnp.sum(second, axis=0, keepdims=True)
    row = lax.broadcasted_iota(jnp.int32, (8, 128), 0)
    kind = lax.rem(row, 4)
    base = jnp.where(
        kind == 0, first[:, 0:128],
        jnp.where(kind == 1, first[:, 128:256], jnp.where(kind == 2, second[:, 0:128], second[:, 128:256])),
    )
    for s in range(8):
        msg_b[s] = jnp.where(2 * s + row // 4 == mine, base, 0.0)
    waits += all_reduce(msg_b, got_b, red_b, sum_y_b, sum_z_b, all_b, as_b, ar_b)
    total = jnp.zeros((8, 128), F32)
    for s in range(8):
        total = total + jnp.where(2 * s + row // 4 == mine, all_b[s], 0.0)

    def pick(i):
        return jnp.sum(jnp.where(kind == i, total, 0.0), axis=0, keepdims=True)

    mean = jnp.concatenate([pick(0), pick(1)], axis=1) / COUNT
    inv = lax.rsqrt(jnp.concatenate([pick(2), pick(3)], axis=1) / COUNT - mean * mean + 1e-05)

    def finish(b, _):
        v = (proj[b] - mean) * inv * pgain[...] + pshift[...]
        v = jnp.maximum(v, 0.0)
        for lane in range(2):
            rows[lane] = v[:, 128 * lane : 128 * (lane + 1)]
            for i in range(3):
                for k in range(2):
                    pair = rows[lane, pl.ds(64 * i + k, 32, stride=2), :]
                    tiles[lane, pl.ds(2 * i + k, 32, stride=8), :] = pair
        both = jnp.concatenate([tiles[0].reshape(32, 8, 128), tiles[1].reshape(32, 8, 128)], axis=1)
        sendbuf[pl.ds(32 * b, 32)] = both.astype(BF16)
        return 0

    tiles[...] = jnp.zeros(tiles.shape, F32)
    lax.fori_loop(0, 4, finish, 0)

    start = own * 32 + d
    slot = image * 2 + c
    pltpu.make_async_copy(sendbuf.at[start], out.at[slot], end_recv).start()

    def scatter(e, _):
        e = lax.rem(start + e, 128)
        remote(
            sendbuf.at[e], out.at[slot], end_send, end_recv, (lax.rem(e, 32), 2 * (e // 32) + parity)
        ).start()
        return 0

    lax.fori_loop(1, 128, scatter, 0)
    for cp in waits:
        cp.wait_send()
    for i in range(2):
        for h in range(2):
            is_self = jnp.logical_and(jnp.logical_and(c == z_hi, c == h), half == i)

            @pl.when(jnp.logical_not(is_self))
            def _():
                src = feat.at[i, pl.ds(3 * h, 3)]
                remote(src, xbuf.at[own], fs.at[2 * i + h], fr.at[own], sibling).wait_send()

    rest = sendbuf.at[pl.ds(0, 127)]
    pltpu.make_async_copy(rest, rest, end_send).wait()
    pltpu.make_async_copy(out, out, end_recv).wait()


def shards(
    features, first_w, second_w, third_w, point_w, pool_w, proj_w, gain, shift, pgain, pshift, group
):
    any_ = pl.BlockSpec(memory_space=pl.ANY)
    vmem = pl.BlockSpec(memory_space=pltpu.VMEM)
    smem = pl.BlockSpec(memory_space=pltpu.SMEM)
    dma = pltpu.SemaphoreType.DMA
    reduce_bufs = [
        pltpu.VMEM((n, rows, 128), F32) for rows in (32, 8) for n in (8, 7, 2, 3, 7, 8)
    ]
    out = pl.pallas_call(
        kernel,
        out_shape=jax.ShapeDtypeStruct((128, 16, 128), BF16),
        in_specs=[any_] * 4 + [vmem] * 7 + [smem],
        out_specs=any_,
        scratch_shapes=[
            pltpu.VMEM((27, 4, 4, 2, 32, 256), BF16),
            pltpu.VMEM((4, 3, 64, 1024), BF16),
            pltpu.VMEM((4, 3, 64, 1024), BF16),
            pltpu.VMEM((4, 3, 64, 1024), BF16),
            pltpu.VMEM((4, 3, 64, 1024), F32),
            pltpu.VMEM((4, 192, 256), F32),
            pltpu.VMEM((2, 192, 128), F32),
            pltpu.VMEM((2, 256, 128), F32),
            pltpu.VMEM((128, 16, 128), BF16),
            pltpu.VMEM((4, 8, 1024), F32),
            *reduce_bufs,
            dma((3,)), dma((CHUNKS, 12)), dma((CHUNKS, 12)), dma((4,)), dma((4,)), dma((3,)), dma((3,)),
            dma((24,)), dma((24,)), dma((24,)), dma((24,)), dma(()), dma(()),
        ],
        compiler_params=pltpu.CompilerParams(
            collective_id=0, has_side_effects=True, vmem_limit_bytes=56 << 20
        ),
        cost_estimate=pl.CostEstimate(flops=8_000_000_000, bytes_accessed=20_000_000, transcendentals=0),
    )(
        features, first_w.reshape(9, 32, 256), second_w.reshape(9, 32, 256), third_w.reshape(9, 32, 256),
        point_w, pool_w, proj_w, gain.reshape(1, -1), shift.reshape(1, -1),
        pgain.reshape(1, -1), pshift.reshape(1, -1), group,
    )
    out = out.reshape(64, 2, 2, 8, 128)[:, :, :, :6].reshape(64, 2, 2, 3, 2, 128)
    return out.transpose(0, 1, 3, 4, 2, 5).reshape(64, 6, 2, 256)


def solution(mesh):
    weight = P(None, None, "dp", None)
    in_specs = (P("dp", "rows", None, None), weight, weight, weight) + (P(),) * 8
    return jax.shard_map(
        shards, mesh=mesh, in_specs=in_specs, out_specs=P(None, "rows", "dp", None), check_vma=False
    )
```

```python
import functools

import jax
import jax.numpy as jnp
from jax import lax
from jax.experimental import pallas as pl
from jax.experimental.pallas import tpu as pltpu
from jax.sharding import PartitionSpec as P

MESH = pl.DeviceIdType.MESH
F32 = jnp.float32
BF16 = jnp.bfloat16
ORDER = ((0, 1), (1, 1), (2, 1), (0, 0), (0, 2), (1, 0), (1, 2), (2, 0), (2, 2))
CHUNKS = len(ORDER)
COUNT = 4.0 * 48 * 64
PIXELS = 48.0 * 64


def device(x, y, z, c):
    x, y, z, c = lax.rem(x + 4, 4), lax.rem(y + 4, 4), lax.rem(z + 8, 8), lax.rem(c, 2)
    return (lax.rem(z, 4) * 8 + x * 2 + c, (z // 4) * 4 + y)


def remote(src, dst, send, recv, to):
    return pltpu.make_async_remote_copy(
        src_ref=src, dst_ref=dst, send_sem=send, recv_sem=recv, device_id=to, device_id_type=MESH
    )


def kernel(
    feat, wa, wb, wc, point_w, pool_w, proj_w, gain, shift, pgain, pshift, group,
    out,
    wbuf, xbuf, xright, xleft, acc, proj, rows, tiles, sendbuf, pool_buf,
    msg_a, got_a, red_a, sum_y_a, sum_z_a, all_a,
    msg_b, got_b, red_b, sum_y_b, sum_z_b, all_b,
    local_sem, ws, wr, fs, fr, ps, pr, as_a, ar_a, as_b, ar_b, end_send, end_recv,
):
    d, r = lax.axis_index("dp"), lax.axis_index("rows")
    z_lo, x, c = d // 8, lax.rem(d // 2, 4), lax.rem(d, 2)
    z_hi, y = r // 4, lax.rem(r, 4)
    z = z_hi * 4 + z_lo
    parity, half = lax.rem(y, 2), y // 2
    own = z_hi * 2 + half
    image = (d // 2) * 4 + own
    other = 1 - c
    y_pair = y + 1 - 2 * parity
    up, down = device(x, y, z + 1, c), device(x, y, z - 1, c)
    right, left = device(x + 1, y, z, c), device(x - 1, y, z, c)
    y_up, y_down = device(x, y + 1, z, c), device(x, y - 1, z, c)
    sibling = device(x, y, z, other)
    pool_peers = (sibling, device(x, y_pair, z, c), device(x, y_pair, z, other))

    locals_ = [
        pltpu.make_async_copy(w, wbuf.at[pl.ds(9 * i, 9), z_lo, x, c], local_sem.at[i])
        for i, w in enumerate((wa, wb, wc))
    ]
    for cp in locals_:
        cp.start()

    barrier = pltpu.get_barrier_semaphore()
    for peer in (up, down, right, left, y_up, y_down, sibling, pool_peers[2]):
        pl.semaphore_signal(barrier, inc=1, device_id=peer, device_id_type=MESH)
    for b in range(4):
        src = device(x, 2 * (b % 2) + parity, (b // 2) * 4 + z_lo, z_hi)

        @pl.when(jnp.logical_not(jnp.logical_and(own == b, c == z_hi)))
        def _():
            pl.semaphore_signal(barrier, inc=1, device_id=src, device_id_type=MESH)

    @pl.when(c == z_hi)
    def _():
        pl.semaphore_wait(barrier, 11)

    @pl.when(c != z_hi)
    def _():
        pl.semaphore_wait(barrier, 12)

    for cp in locals_:
        cp.wait()

    def taps(k):
        b, kh = ORDER[k]
        return pl.ds(9 * b + 3 * kh, 3)

    def shard(k, zz, rows=None):
        ref = wbuf.at[taps(k), zz, x, c]
        return ref if rows is None else wbuf.at[taps(k), zz, x, c, pl.ds(rows, 16)]

    def column(k, xx, cc, zs=None, n=2):
        return wbuf.at[taps(k), slice(None) if zs is None else pl.ds(zs, n), xx, cc]

    z_next, z_prev = lax.rem(z_lo + 1, 4), lax.rem(z_lo + 3, 4)
    z_far = lax.rem(z_lo + 2, 4)
    x_next, x_prev, x_far = lax.rem(x + 1, 4), lax.rem(x + 3, 4), lax.rem(x + 2, 4)

    def to(ref, k, i, peer):
        return remote(ref, ref, ws.at[k, i], wr.at[k, i], peer)

    sent = []

    def send(ref, k, i, peer):
        cp = to(ref, k, i, peer)
        cp.start()
        sent.append(cp)

    def arrived(ref, k, i):
        to(ref, k, i, sibling).wait_recv()

    for k in range(CHUNKS):
        send(shard(k, z_lo), k, 0, up)
        send(shard(k, z_lo), k, 1, down)

    def piece(i, h, row):
        is_self = jnp.logical_and(jnp.logical_and(c == z_hi, c == h), half == i)
        src, dst = feat.at[i, 3 * h + row], xbuf.at[own, row]
        there = device(x, 2 * i + parity, c * 4 + z_lo, jnp.int32(h))
        copy = remote(src, dst, fs.at[2 * i + h, row], fr.at[own, row], there)
        return is_self, copy, lambda: pltpu.make_async_copy(src, dst, fr.at[own, row]).start()

    def send_piece(i, h, row):
        is_self, copy, local = piece(i, h, row)

        @pl.when(is_self)
        def _():
            local()

        @pl.when(jnp.logical_not(is_self))
        def _():
            copy.start()

    pieces = [(i, h, row) for row in range(3) for i in range(2) for h in range(2)]

    def features_arrive():
        for b in range(4):
            for row in range(3):
                pltpu.make_async_copy(xbuf.at[b, row], xbuf.at[b, row], fr.at[b, row]).wait()
        part = jnp.zeros((8, 1024), F32)
        col = lax.broadcasted_iota(jnp.int32, (64, 1024), 0)

        def body(t, part):
            v = xbuf[t // 3, lax.rem(t, 3)].astype(F32)
            xright[t // 3, lax.rem(t, 3)] = jnp.where(col >= 4, pltpu.roll(v, 4, 0), 0.0).astype(BF16)
            xleft[t // 3, lax.rem(t, 3)] = jnp.where(col < 60, pltpu.roll(v, 60, 0), 0.0).astype(BF16)
            return part + v.reshape(8, 8, 1024).sum(axis=0)

        pool_buf[0] = lax.fori_loop(0, 12, body, part)
        for i, peer in enumerate(pool_peers):
            remote(pool_buf.at[0], pool_buf.at[i + 1], ps.at[i], pr.at[i], peer).start()

        def point(b, _):
            acc[b, :, :, 0:256] = jnp.dot(
                xbuf[b].reshape(192, 1024), point_w[...], preferred_element_type=F32
            ).reshape(3, 64, 256)
            return 0

        lax.fori_loop(0, 4, point, 0)

    def compute(k):
        branch, kh = ORDER[k]
        step = branch + 1
        x0 = (0, 0, step)[kh]
        o0 = (step, 0, 0)[kh]
        blocks = 4 if kh == 1 else 4 - step
        lanes = slice(256 * (branch + 1), 256 * (branch + 2))

        def body(t, _):
            b, o = x0 + t, o0 + t

            def times(lhs, kw):
                n = lhs.shape[1]
                w = wbuf[9 * branch + 3 * kh + kw].reshape(1024, 256)
                return jnp.dot(
                    lhs.reshape(3 * n, 1024), w, preferred_element_type=F32
                ).reshape(3, n, 256)

            mid = times(xbuf[b], 1)
            if kh == 1:
                acc[o, :, :, lanes] = mid
            else:
                acc[o, :, :, lanes] += mid
            if branch == 0:
                acc[o, :, 8:64, lanes] += times(xright[b], 0)[:, 0:56]
                acc[o, :, 0:56, lanes] += times(xleft[b], 2)[:, 8:64]
            elif branch == 1:
                acc[o, :, 24:64, lanes] += times(xbuf[b, :, 0:48], 0)[:, 0:40]
                acc[o, :, 0:40, lanes] += times(xbuf[b, :, 16:64], 2)[:, 8:48]
            else:
                acc[o, :, 32:64, lanes] += times(xright[b, :, 0:32], 0)
                acc[o, :, 0:32, lanes] += times(xleft[b, :, 32:64], 2)
            return 0

        lax.fori_loop(0, blocks, body, 0)

    z_own, z_rest = 2 * parity, 2 - 2 * parity
    for t in range(CHUNKS + 5):
        k = t
        if 0 <= k < CHUNKS:
            arrived(shard(k, z_prev), k, 0)
            send(shard(k, z_prev, 16), k, 2, up)
            arrived(shard(k, z_next), k, 1)
            send(shard(k, z_next, 0), k, 3, down)
        k = t - 1
        if 0 <= k < CHUNKS:
            arrived(shard(k, z_far, 16), k, 2)
            arrived(shard(k, z_far, 0), k, 3)
            send(column(k, x, c), k, 4, right)
            send(column(k, x, c), k, 5, left)
            send(column(k, x, c), k, 8, sibling)
        for p in pieces[2 * t : 2 * t + 2]:
            send_piece(*p)
        k = t - 2
        if 0 <= k < CHUNKS:
            arrived(column(k, x_prev, c), k, 4)
            send(column(k, x_prev, c, z_own + 1, 1), k, 6, right)
            arrived(column(k, x_next, c), k, 5)
            send(column(k, x_next, c, z_own, 1), k, 7, left)
            send(column(k, x_prev, c), k, 9, sibling)
            send(column(k, x_next, c), k, 10, sibling)
        k = t - 3
        if 0 <= k < CHUNKS:
            arrived(column(k, x_far, c, z_own + 1, 1), k, 6)
            arrived(column(k, x_far, c, z_own, 1), k, 7)
            send(column(k, x_far, c, z_own, 1), k, 12, y_up)
            send(column(k, x_far, c, z_own + 1, 1), k, 13, y_down)
            send(column(k, x_far, c, z_own), k, 11, sibling)
        k = t - 4
        if 0 <= k < CHUNKS:
            arrived(column(k, x_far, c, z_rest, 1), k, 12)
            arrived(column(k, x_far, c, z_rest + 1, 1), k, 13)
            send(column(k, x_far, c, z_rest), k, 14, sibling)
        if t == 8:
            features_arrive()
        for k in (2 * (t - 9), 2 * (t - 9) + 1):
            if 0 <= k < CHUNKS:
                arrived(column(k, x, other), k, 8)
                arrived(column(k, x_prev, other), k, 9)
                arrived(column(k, x_next, other), k, 10)
                arrived(column(k, x_far, other, z_own), k, 11)
                arrived(column(k, x_far, other, z_rest), k, 14)
                compute(k)

    for cp in sent:
        cp.wait_send()

    mine = group[image]
    spot = x * 2 + c

    def all_reduce(msg, got, red, sum_y, sum_z, full, s_sem, r_sem):
        def peer(o):
            s = lax.rem(spot + o, 8)
            return s, device(s // 2, y, z, lax.rem(s, 2))

        copies = []

        def go(src, dst, i, to_):
            cp = remote(src, dst, s_sem.at[i], r_sem.at[i], to_)
            cp.start()
            copies.append(cp)

        for o in range(1, 8):
            s, to_ = peer(o)
            go(msg.at[s], got.at[o - 1], o - 1, to_)
        total = msg[spot]
        for o in range(1, 8):
            copies[o - 1].wait_recv()
            total = total + got[o - 1]
        red[0] = total
        for o in range(1, 4):
            go(red.at[0], sum_y.at[o - 1], 6 + o, device(x, y + o, z, c))
        for o in range(1, 4):
            copies[6 + o].wait_recv()
            total = total + sum_y[o - 1]
        red[1] = total
        for o in range(1, 8):
            go(red.at[1], sum_z.at[o - 1], 9 + o, device(x, y, z + o, c))
        for o in range(1, 8):
            copies[9 + o].wait_recv()
            total = total + sum_z[o - 1]
        full[spot] = total
        for o in range(1, 8):
            s, to_ = peer(o)
            go(full.at[spot], full.at[spot], 16 + o, to_)
        for o in range(1, 8):
            s = lax.rem(spot - o + 8, 8)
            remote(full.at[s], full.at[s], s_sem.at[16 + o], r_sem.at[16 + o], sibling).wait_recv()
        return copies

    def add_up(t, carry):
        first, second = carry
        v = acc[t // 3, lax.rem(t, 3)].reshape(8, 8, 1024)
        return first + v.sum(axis=0), second + (v * v).sum(axis=0)

    zero = jnp.zeros((8, 1024), F32)
    first, second = lax.fori_loop(0, 12, add_up, (zero, zero))
    first = jnp.sum(first, axis=0, keepdims=True)
    second = jnp.sum(second, axis=0, keepdims=True)
    labels = lax.broadcasted_iota(jnp.int32, (16, 128), 0)
    for s in range(8):
        lanes = slice(128 * s, 128 * (s + 1))
        msg_a[s, 0:16] = jnp.where(labels == mine, first[:, lanes], 0.0)
        msg_a[s, 16:32] = jnp.where(labels == mine, second[:, lanes], 0.0)
    waits = all_reduce(msg_a, got_a, red_a, sum_y_a, sum_z_a, all_a, as_a, ar_a)

    means, invs = [], []
    for s in range(8):
        g1 = jnp.sum(jnp.where(labels == mine, all_a[s, 0:16], 0.0), axis=0, keepdims=True)
        g2 = jnp.sum(jnp.where(labels == mine, all_a[s, 16:32], 0.0), axis=0, keepdims=True)
        mean = g1 / COUNT
        means.append(mean)
        invs.append(lax.rsqrt(g2 / COUNT - mean * mean + 1e-05))
    mean = jnp.concatenate(means, axis=1)
    inv = jnp.concatenate(invs, axis=1)

    for i in range(3):
        remote(pool_buf.at[i + 1], pool_buf.at[i + 1], ps.at[i], pr.at[i], sibling).wait()
    pool = pool_buf[0] + pool_buf[1] + pool_buf[2] + pool_buf[3]
    pooled = (jnp.sum(pool, axis=0, keepdims=True) / PIXELS).astype(BF16)
    pooled = jnp.broadcast_to(pooled, (16, 1024))
    act = jnp.maximum(jnp.dot(pooled, pool_w[...], preferred_element_type=F32), 0.0).astype(BF16)
    pool_row = jnp.dot(act, proj_w[1024:1280], preferred_element_type=F32)[0:1]

    gains = jnp.concatenate([gain[i : i + 1] for i in range(4)], axis=1)
    shifts = jnp.concatenate([shift[i : i + 1] for i in range(4)], axis=1)

    def project(b, carry):
        first, second = carry
        v = acc[b].reshape(192, 1024)
        v = (v - mean) * inv * gains + shifts
        v = jnp.maximum(v, 0.0).astype(BF16)
        p = jnp.dot(v, proj_w[0:1024], preferred_element_type=F32) + pool_row
        proj[b] = p
        p = p.reshape(24, 8, 256)
        return first + p.sum(axis=0), second + (p * p).sum(axis=0)

    zero = jnp.zeros((8, 256), F32)
    first, second = lax.fori_loop(0, 4, project, (zero, zero))
    first = jnp.sum(first, axis=0, keepdims=True)
    second = jnp.sum(second, axis=0, keepdims=True)
    row = lax.broadcasted_iota(jnp.int32, (8, 128), 0)
    kind = lax.rem(row, 4)
    base = jnp.where(
        kind == 0, first[:, 0:128],
        jnp.where(kind == 1, first[:, 128:256], jnp.where(kind == 2, second[:, 0:128], second[:, 128:256])),
    )
    for s in range(8):
        msg_b[s] = jnp.where(2 * s + row // 4 == mine, base, 0.0)
    waits += all_reduce(msg_b, got_b, red_b, sum_y_b, sum_z_b, all_b, as_b, ar_b)
    total = jnp.zeros((8, 128), F32)
    for s in range(8):
        total = total + jnp.where(2 * s + row // 4 == mine, all_b[s], 0.0)

    def pick(i):
        return jnp.sum(jnp.where(kind == i, total, 0.0), axis=0, keepdims=True)

    mean = jnp.concatenate([pick(0), pick(1)], axis=1) / COUNT
    inv = lax.rsqrt(jnp.concatenate([pick(2), pick(3)], axis=1) / COUNT - mean * mean + 1e-05)

    def finish(b, _):
        v = (proj[b] - mean) * inv * pgain[...] + pshift[...]
        v = jnp.maximum(v, 0.0)
        for lane in range(2):
            rows[lane] = v[:, 128 * lane : 128 * (lane + 1)]
            for i in range(3):
                for k in range(2):
                    pair = rows[lane, pl.ds(64 * i + k, 32, stride=2), :]
                    tiles[lane, pl.ds(2 * i + k, 32, stride=8), :] = pair
        both = jnp.concatenate([tiles[0].reshape(32, 8, 128), tiles[1].reshape(32, 8, 128)], axis=1)
        sendbuf[pl.ds(32 * b, 32)] = both.astype(BF16)
        return 0

    tiles[...] = jnp.zeros(tiles.shape, F32)
    lax.fori_loop(0, 4, finish, 0)

    start = own * 32 + d
    slot = image * 2 + c
    pltpu.make_async_copy(sendbuf.at[start], out.at[slot], end_recv).start()

    def scatter(e, _):
        e = lax.rem(start + e, 128)
        remote(
            sendbuf.at[e], out.at[slot], end_send, end_recv, (lax.rem(e, 32), 2 * (e // 32) + parity)
        ).start()
        return 0

    lax.fori_loop(1, 128, scatter, 0)
    for cp in waits:
        cp.wait_send()
    for p in pieces:
        is_self, copy, _ = piece(*p)

        @pl.when(jnp.logical_not(is_self))
        def _():
            copy.wait_send()

    rest = sendbuf.at[pl.ds(0, 127)]
    pltpu.make_async_copy(rest, rest, end_send).wait()
    pltpu.make_async_copy(out, out, end_recv).wait()


def shards(
    features, first_w, second_w, third_w, point_w, pool_w, proj_w, gain, shift, pgain, pshift, group
):
    any_ = pl.BlockSpec(memory_space=pl.ANY)
    vmem = pl.BlockSpec(memory_space=pltpu.VMEM)
    smem = pl.BlockSpec(memory_space=pltpu.SMEM)
    dma = pltpu.SemaphoreType.DMA
    reduce_bufs = [
        pltpu.VMEM((n, rows, 128), F32) for rows in (32, 8) for n in (8, 7, 2, 3, 7, 8)
    ]
    out = pl.pallas_call(
        kernel,
        out_shape=jax.ShapeDtypeStruct((128, 16, 128), BF16),
        in_specs=[any_] * 4 + [vmem] * 7 + [smem],
        out_specs=any_,
        scratch_shapes=[
            pltpu.VMEM((27, 4, 4, 2, 32, 256), BF16),
            pltpu.VMEM((4, 3, 64, 1024), BF16),
            pltpu.VMEM((4, 3, 64, 1024), BF16),
            pltpu.VMEM((4, 3, 64, 1024), BF16),
            pltpu.VMEM((4, 3, 64, 1024), F32),
            pltpu.VMEM((4, 192, 256), F32),
            pltpu.VMEM((2, 192, 128), F32),
            pltpu.VMEM((2, 256, 128), F32),
            pltpu.VMEM((128, 16, 128), BF16),
            pltpu.VMEM((4, 8, 1024), F32),
            *reduce_bufs,
            dma((3,)), dma((CHUNKS, 15)), dma((CHUNKS, 15)), dma((4, 3)), dma((4, 3)), dma((3,)), dma((3,)),
            dma((24,)), dma((24,)), dma((24,)), dma((24,)), dma(()), dma(()),
        ],
        compiler_params=pltpu.CompilerParams(
            collective_id=0, has_side_effects=True, vmem_limit_bytes=56 << 20
        ),
        cost_estimate=pl.CostEstimate(flops=8_000_000_000, bytes_accessed=20_000_000, transcendentals=0),
    )(
        features, first_w.reshape(9, 32, 256), second_w.reshape(9, 32, 256), third_w.reshape(9, 32, 256),
        point_w, pool_w, proj_w, gain, shift,
        pgain.reshape(1, -1), pshift.reshape(1, -1), group,
    )
    out = out.reshape(64, 2, 2, 8, 128)[:, :, :, :6].reshape(64, 2, 2, 3, 2, 128)
    return out.transpose(0, 1, 3, 4, 2, 5).reshape(64, 6, 2, 256)


def solution(mesh):
    weight = P(None, None, "dp", None)
    in_specs = (P("dp", "rows", None, None), weight, weight, weight) + (P(),) * 8
    return jax.shard_map(
        shards, mesh=mesh, in_specs=in_specs, out_specs=P(None, "rows", "dp", None), check_vma=False
    )
```

```python
import functools

import jax
import jax.numpy as jnp
from jax import lax
from jax.experimental import pallas as pl
from jax.experimental.pallas import tpu as pltpu
from jax.sharding import PartitionSpec as P

MESH = pl.DeviceIdType.MESH
F32 = jnp.float32
BF16 = jnp.bfloat16
ORDER = ((0, 1), (1, 1), (2, 1), (0, 0), (0, 2), (1, 0), (1, 2), (2, 0), (2, 2))
CHUNKS = len(ORDER)
AHEAD = 4
PER_STEP = (1, 1, 1, 1, 1, 2, 2, 2, 1)
WORK = {
    8: ((0, 1), ((0, 0, 2),)),
    9: ((), ((1, 0, 2), (2, 0, 2))),
    10: ((), ((3, 0, 2), (4, 0, 2))),
    11: ((2,), ((0, 2, 1), (1, 2, 1))),
    12: ((), ((2, 2, 1), (3, 2, 1), (4, 2, 1), (5, 0, 3), (6, 0, 3))),
    13: ((), ((7, 0, 3), (8, 0, 3))),
}
COUNT = 4.0 * 48 * 64
PIXELS = 48.0 * 64


def device(x, y, z, c):
    x, y, z, c = lax.rem(x + 4, 4), lax.rem(y + 4, 4), lax.rem(z + 8, 8), lax.rem(c, 2)
    return (lax.rem(z, 4) * 8 + x * 2 + c, (z // 4) * 4 + y)


def remote(src, dst, send, recv, to):
    return pltpu.make_async_remote_copy(
        src_ref=src, dst_ref=dst, send_sem=send, recv_sem=recv, device_id=to, device_id_type=MESH
    )


def kernel(
    feat, wa, wb, wc, point_w, pool_w, proj_w, gain, shift, pgain, pshift, group,
    out,
    wbuf, xbuf, xright, xleft, acc, proj, halves, tiles, sendbuf, pool_buf,
    msg_a, got_a, red_a, sum_y_a, sum_z_a, all_a,
    msg_b, got_b, red_b, sum_y_b, sum_z_b, all_b,
    local_sem, ws, wr, fs, fr, ps, pr, as_a, ar_a, as_b, ar_b, end_send, end_recv,
):
    d, r = lax.axis_index("dp"), lax.axis_index("rows")
    z_lo, x, c = d // 8, lax.rem(d // 2, 4), lax.rem(d, 2)
    z_hi, y = r // 4, lax.rem(r, 4)
    z = z_hi * 4 + z_lo
    parity, half = lax.rem(y, 2), y // 2
    own = z_hi * 2 + half
    image = (d // 2) * 4 + own
    other = 1 - c
    y_pair = y + 1 - 2 * parity
    up, down = device(x, y, z + 1, c), device(x, y, z - 1, c)
    right, left = device(x + 1, y, z, c), device(x - 1, y, z, c)
    y_up, y_down = device(x, y + 1, z, c), device(x, y - 1, z, c)
    sibling = device(x, y, z, other)
    pool_peers = (sibling, device(x, y_pair, z, c), device(x, y_pair, z, other))

    locals_ = [
        pltpu.make_async_copy(w, wbuf.at[pl.ds(9 * i, 9), z_lo, x, c], local_sem.at[i])
        for i, w in enumerate((wa, wb, wc))
    ]
    for cp in locals_:
        cp.start()

    barrier = pltpu.get_barrier_semaphore()
    for peer in (up, down, right, left, y_up, y_down, sibling, pool_peers[2]):
        pl.semaphore_signal(barrier, inc=1, device_id=peer, device_id_type=MESH)
    for b in range(4):
        src = device(x, 2 * (b % 2) + parity, (b // 2) * 4 + z_lo, z_hi)

        @pl.when(jnp.logical_not(jnp.logical_and(own == b, c == z_hi)))
        def _():
            pl.semaphore_signal(barrier, inc=1, device_id=src, device_id_type=MESH)

    @pl.when(c == z_hi)
    def _():
        pl.semaphore_wait(barrier, 11)

    @pl.when(c != z_hi)
    def _():
        pl.semaphore_wait(barrier, 12)

    for cp in locals_:
        cp.wait()

    def taps(k):
        b, kh = ORDER[k]
        return pl.ds(9 * b + 3 * kh, 3)

    def shard(k, zz, rows=None):
        ref = wbuf.at[taps(k), zz, x, c]
        return ref if rows is None else wbuf.at[taps(k), zz, x, c, pl.ds(rows, 16)]

    def column(k, xx, cc, zs=None, n=2):
        return wbuf.at[taps(k), slice(None) if zs is None else pl.ds(zs, n), xx, cc]

    def whole(k, cc):
        return wbuf.at[taps(k), :, :, cc]

    z_next, z_prev = lax.rem(z_lo + 1, 4), lax.rem(z_lo + 3, 4)
    z_far = lax.rem(z_lo + 2, 4)
    x_next, x_prev, x_far = lax.rem(x + 1, 4), lax.rem(x + 3, 4), lax.rem(x + 2, 4)

    def to(ref, k, i, peer):
        return remote(ref, ref, ws.at[k, i], wr.at[k, i], peer)

    sent = []

    def send(ref, k, i, peer):
        cp = to(ref, k, i, peer)
        cp.start()
        sent.append(cp)

    def arrived(ref, k, i):
        to(ref, k, i, sibling).wait_recv()

    def send_own(k):
        send(shard(k, z_lo), k, 0, up)
        send(shard(k, z_lo), k, 1, down)

    for k in range(AHEAD):
        send_own(k)

    def piece(i, h, row):
        is_self = jnp.logical_and(jnp.logical_and(c == z_hi, c == h), half == i)
        src, dst = feat.at[i, 3 * h + row], xbuf.at[own, row]
        there = device(x, 2 * i + parity, c * 4 + z_lo, jnp.int32(h))
        copy = remote(src, dst, fs.at[2 * i + h, row], fr.at[own, row], there)
        return is_self, copy, lambda: pltpu.make_async_copy(src, dst, fr.at[own, row]).start()

    def send_piece(i, h, row):
        is_self, copy, local = piece(i, h, row)

        @pl.when(is_self)
        def _():
            local()

        @pl.when(jnp.logical_not(is_self))
        def _():
            copy.start()

    pieces = [(i, h, row) for row in range(3) for i in range(2) for h in range(2)]

    col = lax.broadcasted_iota(jnp.int32, (64, 1024), 0)

    def features_arrive(arriving):
        first, count = arriving[0], len(arriving)
        for b in range(4):
            for row in arriving:
                pltpu.make_async_copy(xbuf.at[b, row], xbuf.at[b, row], fr.at[b, row]).wait()

        def body(b, part):
            for row in arriving:
                v = xbuf[b, row].astype(F32)
                xright[b, row] = jnp.where(col >= 4, pltpu.roll(v, 4, 0), 0.0).astype(BF16)
                xleft[b, row] = jnp.where(col < 60, pltpu.roll(v, 60, 0), 0.0).astype(BF16)
                part = part + v.reshape(8, 8, 1024).sum(axis=0)
            return part

        part = jnp.zeros((8, 1024), F32) if first == 0 else pool_buf[0]
        pool_buf[0] = lax.fori_loop(0, 4, body, part)
        if arriving[-1] == 2:
            for i, peer in enumerate(pool_peers):
                remote(pool_buf.at[0], pool_buf.at[i + 1], ps.at[i], pr.at[i], peer).start()
        acc[:, first : first + count, :, 0:256] = jnp.dot(
            xbuf[:, first : first + count].reshape(count * 256, 1024), point_w[...],
            preferred_element_type=F32,
        ).reshape(4, count, 64, 256)

    def compute(k, row, rows):
        branch, kh = ORDER[k]
        step = branch + 1
        n = 4 if kh == 1 else 4 - step
        src = (pl.ds((0, 0, step)[kh], n), pl.ds(row, rows))
        dst = (pl.ds((step, 0, 0)[kh], n), pl.ds(row, rows))
        lanes = pl.ds(256 * (branch + 1), 256)

        def times(lhs, kw):
            m = lhs.shape[2]
            w = wbuf[9 * branch + 3 * kh + kw].reshape(1024, 256)
            return jnp.dot(
                lhs.reshape(n * rows * m, 1024), w, preferred_element_type=F32
            ).reshape(n, rows, m, 256)

        mid = times(xbuf[src], 1)
        if kh == 1:
            acc[*dst, :, lanes] = mid
        else:
            acc[*dst, :, lanes] += mid
        if branch == 0:
            acc[*dst, 8:64, lanes] += times(xright[src], 0)[:, :, 0:56]
            acc[*dst, 0:56, lanes] += times(xleft[src], 2)[:, :, 8:64]
        elif branch == 1:
            acc[*dst, 24:64, lanes] += times(xbuf[*src, 0:48], 0)[:, :, 0:40]
            acc[*dst, 0:40, lanes] += times(xbuf[*src, 16:64], 2)[:, :, 8:48]
        else:
            acc[*dst, 32:64, lanes] += times(xright[*src, 0:32], 0)
            acc[*dst, 0:32, lanes] += times(xleft[*src, 32:64], 2)

    here = set()
    z_own, z_rest = 2 * parity, 2 - 2 * parity
    for t in range(CHUNKS + 5):
        for k in (2 * t, 2 * t + 1):
            if k < CHUNKS:
                arrived(shard(k, z_prev), k, 0)
                send(shard(k, z_prev, 16), k, 2, up)
                arrived(shard(k, z_next), k, 1)
                send(shard(k, z_next, 0), k, 3, down)
            if k + AHEAD < CHUNKS:
                send_own(k + AHEAD)
        k = t - 1
        if 0 <= k < CHUNKS:
            arrived(shard(k, z_far, 16), k, 2)
            arrived(shard(k, z_far, 0), k, 3)
            send(column(k, x, c), k, 4, right)
            send(column(k, x, c), k, 5, left)
        done = sum(PER_STEP[:t])
        for p in pieces[done : done + sum(PER_STEP[t : t + 1])]:
            send_piece(*p)
        k = t - 2
        if 0 <= k < CHUNKS:
            arrived(column(k, x_prev, c), k, 4)
            send(column(k, x_prev, c, z_own + 1, 1), k, 6, right)
            arrived(column(k, x_next, c), k, 5)
            send(column(k, x_next, c, z_own, 1), k, 7, left)
        k = t - 3
        if 0 <= k < CHUNKS:
            arrived(column(k, x_far, c, z_own + 1, 1), k, 6)
            arrived(column(k, x_far, c, z_own, 1), k, 7)
            send(column(k, x_far, c, z_own, 1), k, 9, y_up)
            send(column(k, x_far, c, z_own + 1, 1), k, 10, y_down)
        k = t - 4
        if 0 <= k < CHUNKS:
            arrived(column(k, x_far, c, z_rest, 1), k, 9)
            arrived(column(k, x_far, c, z_rest + 1, 1), k, 10)
            send(whole(k, c), k, 8, sibling)
        arriving, work = WORK.get(t, ((), ()))
        if arriving:
            features_arrive(arriving)
        for k, row, rows in work:
            if k not in here:
                here.add(k)
                arrived(whole(k, other), k, 8)
            compute(k, row, rows)

    for cp in sent:
        cp.wait_send()

    mine = group[image]
    spot = x * 2 + c

    def all_reduce(msg, got, red, sum_y, sum_z, full, s_sem, r_sem):
        def peer(o):
            s = lax.rem(spot + o, 8)
            return s, device(s // 2, y, z, lax.rem(s, 2))

        copies = []

        def go(src, dst, i, to_):
            cp = remote(src, dst, s_sem.at[i], r_sem.at[i], to_)
            cp.start()
            copies.append(cp)

        for o in range(1, 8):
            s, to_ = peer(o)
            go(msg.at[s], got.at[o - 1], o - 1, to_)
        total = msg[spot]
        for o in range(1, 8):
            copies[o - 1].wait_recv()
            total = total + got[o - 1]
        red[0] = total
        for o in range(1, 4):
            go(red.at[0], sum_y.at[o - 1], 6 + o, device(x, y + o, z, c))
        for o in range(1, 4):
            copies[6 + o].wait_recv()
            total = total + sum_y[o - 1]
        red[1] = total
        for o in range(1, 8):
            go(red.at[1], sum_z.at[o - 1], 9 + o, device(x, y, z + o, c))
        for o in range(1, 8):
            copies[9 + o].wait_recv()
            total = total + sum_z[o - 1]
        full[spot] = total
        for o in range(1, 8):
            s, to_ = peer(o)
            go(full.at[spot], full.at[spot], 16 + o, to_)
        for o in range(1, 8):
            s = lax.rem(spot - o + 8, 8)
            remote(full.at[s], full.at[s], s_sem.at[16 + o], r_sem.at[16 + o], sibling).wait_recv()
        return copies

    def add_up(t, carry):
        first, second = carry
        v = acc[t // 3, lax.rem(t, 3)].reshape(8, 8, 1024)
        return first + v.sum(axis=0), second + (v * v).sum(axis=0)

    zero = jnp.zeros((8, 1024), F32)
    first, second = lax.fori_loop(0, 12, add_up, (zero, zero))
    first = jnp.sum(first, axis=0, keepdims=True)
    second = jnp.sum(second, axis=0, keepdims=True)
    labels = lax.broadcasted_iota(jnp.int32, (16, 128), 0)
    for s in range(8):
        lanes = slice(128 * s, 128 * (s + 1))
        msg_a[s, 0:16] = jnp.where(labels == mine, first[:, lanes], 0.0)
        msg_a[s, 16:32] = jnp.where(labels == mine, second[:, lanes], 0.0)
    waits = all_reduce(msg_a, got_a, red_a, sum_y_a, sum_z_a, all_a, as_a, ar_a)

    means, invs = [], []
    for s in range(8):
        g1 = jnp.sum(jnp.where(labels == mine, all_a[s, 0:16], 0.0), axis=0, keepdims=True)
        g2 = jnp.sum(jnp.where(labels == mine, all_a[s, 16:32], 0.0), axis=0, keepdims=True)
        mean = g1 / COUNT
        means.append(mean)
        invs.append(lax.rsqrt(g2 / COUNT - mean * mean + 1e-05))
    mean = jnp.concatenate(means, axis=1)
    inv = jnp.concatenate(invs, axis=1)

    for i in range(3):
        remote(pool_buf.at[i + 1], pool_buf.at[i + 1], ps.at[i], pr.at[i], sibling).wait()
    pool = pool_buf[0] + pool_buf[1] + pool_buf[2] + pool_buf[3]
    pooled = (jnp.sum(pool, axis=0, keepdims=True) / PIXELS).astype(BF16)
    pooled = jnp.broadcast_to(pooled, (16, 1024))
    act = jnp.maximum(jnp.dot(pooled, pool_w[...], preferred_element_type=F32), 0.0).astype(BF16)
    pool_row = jnp.dot(act, proj_w[1024:1280], preferred_element_type=F32)[0:1]

    gains = jnp.concatenate([gain[i : i + 1] for i in range(4)], axis=1)
    shifts = jnp.concatenate([shift[i : i + 1] for i in range(4)], axis=1)

    def project(b, carry):
        first, second = carry
        v = acc[b].reshape(192, 1024)
        v = (v - mean) * inv * gains + shifts
        v = jnp.maximum(v, 0.0).astype(BF16)
        p = jnp.dot(v, proj_w[0:1024], preferred_element_type=F32) + pool_row
        proj[b] = p
        p = p.reshape(24, 8, 256)
        return first + p.sum(axis=0), second + (p * p).sum(axis=0)

    zero = jnp.zeros((8, 256), F32)
    first, second = lax.fori_loop(0, 4, project, (zero, zero))
    first = jnp.sum(first, axis=0, keepdims=True)
    second = jnp.sum(second, axis=0, keepdims=True)
    row = lax.broadcasted_iota(jnp.int32, (8, 128), 0)
    kind = lax.rem(row, 4)
    base = jnp.where(
        kind == 0, first[:, 0:128],
        jnp.where(kind == 1, first[:, 128:256], jnp.where(kind == 2, second[:, 0:128], second[:, 128:256])),
    )
    for s in range(8):
        msg_b[s] = jnp.where(2 * s + row // 4 == mine, base, 0.0)
    waits += all_reduce(msg_b, got_b, red_b, sum_y_b, sum_z_b, all_b, as_b, ar_b)
    total = jnp.zeros((8, 128), F32)
    for s in range(8):
        total = total + jnp.where(2 * s + row // 4 == mine, all_b[s], 0.0)

    def pick(i):
        return jnp.sum(jnp.where(kind == i, total, 0.0), axis=0, keepdims=True)

    mean = jnp.concatenate([pick(0), pick(1)], axis=1) / COUNT
    inv = lax.rsqrt(jnp.concatenate([pick(2), pick(3)], axis=1) / COUNT - mean * mean + 1e-05)

    def finish(b, _):
        v = (proj[b] - mean) * inv * pgain[...] + pshift[...]
        v = jnp.maximum(v, 0.0)
        for lane in range(2):
            halves[lane] = v[:, 128 * lane : 128 * (lane + 1)]
            for i in range(3):
                for k in range(2):
                    pair = halves[lane, pl.ds(64 * i + k, 32, stride=2), :]
                    tiles[lane, pl.ds(2 * i + k, 32, stride=8), :] = pair
        both = jnp.concatenate([tiles[0].reshape(32, 8, 128), tiles[1].reshape(32, 8, 128)], axis=1)
        sendbuf[pl.ds(32 * b, 32)] = both.astype(BF16)
        return 0

    tiles[...] = jnp.zeros(tiles.shape, F32)
    lax.fori_loop(0, 4, finish, 0)

    start = own * 32 + d
    slot = image * 2 + c
    pltpu.make_async_copy(sendbuf.at[start], out.at[slot], end_recv).start()

    def scatter(e, _):
        e = lax.rem(start + e, 128)
        remote(
            sendbuf.at[e], out.at[slot], end_send, end_recv, (lax.rem(e, 32), 2 * (e // 32) + parity)
        ).start()
        return 0

    lax.fori_loop(1, 128, scatter, 0)
    for cp in waits:
        cp.wait_send()
    for p in pieces:
        is_self, copy, _ = piece(*p)

        @pl.when(jnp.logical_not(is_self))
        def _():
            copy.wait_send()

    rest = sendbuf.at[pl.ds(0, 127)]
    pltpu.make_async_copy(rest, rest, end_send).wait()
    pltpu.make_async_copy(out, out, end_recv).wait()


def shards(
    features, first_w, second_w, third_w, point_w, pool_w, proj_w, gain, shift, pgain, pshift, group
):
    any_ = pl.BlockSpec(memory_space=pl.ANY)
    vmem = pl.BlockSpec(memory_space=pltpu.VMEM)
    smem = pl.BlockSpec(memory_space=pltpu.SMEM)
    dma = pltpu.SemaphoreType.DMA
    reduce_bufs = [
        pltpu.VMEM((n, rows, 128), F32) for rows in (32, 8) for n in (8, 7, 2, 3, 7, 8)
    ]
    out = pl.pallas_call(
        kernel,
        out_shape=jax.ShapeDtypeStruct((128, 16, 128), BF16),
        in_specs=[any_] * 4 + [vmem] * 7 + [smem],
        out_specs=any_,
        scratch_shapes=[
            pltpu.VMEM((27, 4, 4, 2, 32, 256), BF16),
            pltpu.VMEM((4, 3, 64, 1024), BF16),
            pltpu.VMEM((4, 3, 64, 1024), BF16),
            pltpu.VMEM((4, 3, 64, 1024), BF16),
            pltpu.VMEM((4, 3, 64, 1024), F32),
            pltpu.VMEM((4, 192, 256), F32),
            pltpu.VMEM((2, 192, 128), F32),
            pltpu.VMEM((2, 256, 128), F32),
            pltpu.VMEM((128, 16, 128), BF16),
            pltpu.VMEM((4, 8, 1024), F32),
            *reduce_bufs,
            dma((3,)), dma((CHUNKS, 11)), dma((CHUNKS, 11)), dma((4, 3)), dma((4, 3)), dma((3,)), dma((3,)),
            dma((24,)), dma((24,)), dma((24,)), dma((24,)), dma(()), dma(()),
        ],
        compiler_params=pltpu.CompilerParams(
            collective_id=0, has_side_effects=True, vmem_limit_bytes=56 << 20
        ),
        cost_estimate=pl.CostEstimate(flops=8_000_000_000, bytes_accessed=20_000_000, transcendentals=0),
    )(
        features, first_w.reshape(9, 32, 256), second_w.reshape(9, 32, 256), third_w.reshape(9, 32, 256),
        point_w, pool_w, proj_w, gain, shift,
        pgain.reshape(1, -1), pshift.reshape(1, -1), group,
    )
    out = out.reshape(64, 2, 2, 8, 128)[:, :, :, :6].reshape(64, 2, 2, 3, 2, 128)
    return out.transpose(0, 1, 3, 4, 2, 5).reshape(64, 6, 2, 256)


def solution(mesh):
    weight = P(None, None, "dp", None)
    in_specs = (P("dp", "rows", None, None), weight, weight, weight) + (P(),) * 8
    return jax.shard_map(
        shards, mesh=mesh, in_specs=in_specs, out_specs=P(None, "rows", "dp", None), check_vma=False
    )
```

```python
import functools

import jax
import jax.numpy as jnp
from jax import lax
from jax.experimental import pallas as pl
from jax.experimental.pallas import tpu as pltpu
from jax.sharding import PartitionSpec as P

MESH = pl.DeviceIdType.MESH
F32 = jnp.float32
BF16 = jnp.bfloat16
ORDER = ((0, 1), (1, 1), (2, 1), (0, 0), (0, 2), (1, 0), (1, 2), (2, 0), (2, 2))
CHUNKS = len(ORDER)
AHEAD = 6
PER_STEP = (1, 1, 1, 1, 1, 2, 2, 2, 1)
WORK = {
    8: ((0, 1), ((0, 0, 2),)),
    9: ((), ((1, 0, 2), (2, 0, 2))),
    10: ((), ((3, 0, 2), (4, 0, 2))),
    11: ((2,), ((0, 2, 1), (1, 2, 1))),
    12: ((), ((2, 2, 1), (3, 2, 1), (4, 2, 1), (5, 0, 3), (6, 0, 3))),
    13: ((), ((7, 0, 3), (8, 0, 3))),
}
COUNT = 4.0 * 48 * 64
PIXELS = 48.0 * 64


def device(x, y, z, c):
    x, y, z, c = lax.rem(x + 4, 4), lax.rem(y + 4, 4), lax.rem(z + 8, 8), lax.rem(c, 2)
    return (lax.rem(z, 4) * 8 + x * 2 + c, (z // 4) * 4 + y)


def remote(src, dst, send, recv, to):
    return pltpu.make_async_remote_copy(
        src_ref=src, dst_ref=dst, send_sem=send, recv_sem=recv, device_id=to, device_id_type=MESH
    )


def kernel(
    feat, wa, wb, wc, point_hbm, pool_hbm, proj_hbm, gain, shift, pgain, pshift, group,
    out,
    wbuf, point_w, pool_w, proj_w, xbuf, xright, xleft, acc, proj, halves, tiles, sendbuf, pool_buf,
    msg_a, got_a, red_a, sum_y_a, sum_z_a, all_a,
    msg_b, got_b, red_b, sum_y_b, sum_z_b, all_b,
    local_sem, ws, wr, fs, fr, ps, pr, as_a, ar_a, as_b, ar_b, end_send, end_recv,
):
    d, r = lax.axis_index("dp"), lax.axis_index("rows")
    z_lo, x, c = d // 8, lax.rem(d // 2, 4), lax.rem(d, 2)
    z_hi, y = r // 4, lax.rem(r, 4)
    z = z_hi * 4 + z_lo
    parity, half = lax.rem(y, 2), y // 2
    own = z_hi * 2 + half
    image = (d // 2) * 4 + own
    other = 1 - c
    y_pair = y + 1 - 2 * parity
    up, down = device(x, y, z + 1, c), device(x, y, z - 1, c)
    right, left = device(x + 1, y, z, c), device(x - 1, y, z, c)
    y_up, y_down = device(x, y + 1, z, c), device(x, y - 1, z, c)
    sibling = device(x, y, z, other)
    pool_peers = (sibling, device(x, y_pair, z, c), device(x, y_pair, z, other))

    locals_ = [
        pltpu.make_async_copy(w, wbuf.at[pl.ds(9 * i, 9), z_lo, x, c], local_sem.at[i])
        for i, w in enumerate((wa, wb, wc))
    ]
    dense = [
        pltpu.make_async_copy(src, dst, local_sem.at[3 + i])
        for i, (src, dst) in enumerate(((point_hbm, point_w), (pool_hbm, pool_w), (proj_hbm, proj_w)))
    ]
    for cp in locals_ + dense:
        cp.start()

    tiles[...] = jnp.zeros(tiles.shape, F32)
    barrier = pltpu.get_barrier_semaphore()
    for peer in (up, down, right, left, y_up, y_down, sibling, pool_peers[2]):
        pl.semaphore_signal(barrier, inc=1, device_id=peer, device_id_type=MESH)
    for b in range(4):
        src = device(x, 2 * (b % 2) + parity, (b // 2) * 4 + z_lo, z_hi)

        @pl.when(jnp.logical_not(jnp.logical_and(own == b, c == z_hi)))
        def _():
            pl.semaphore_signal(barrier, inc=1, device_id=src, device_id_type=MESH)

    @pl.when(c == z_hi)
    def _():
        pl.semaphore_wait(barrier, 11)

    @pl.when(c != z_hi)
    def _():
        pl.semaphore_wait(barrier, 12)

    for cp in locals_:
        cp.wait()

    def taps(k):
        b, kh = ORDER[k]
        return pl.ds(9 * b + 3 * kh, 3)

    def shard(k, zz, rows=None):
        ref = wbuf.at[taps(k), zz, x, c]
        return ref if rows is None else wbuf.at[taps(k), zz, x, c, pl.ds(rows, 16)]

    def column(k, xx, cc, zs=None, n=2):
        return wbuf.at[taps(k), slice(None) if zs is None else pl.ds(zs, n), xx, cc]

    def whole(k, cc):
        return wbuf.at[taps(k), :, :, cc]

    z_next, z_prev = lax.rem(z_lo + 1, 4), lax.rem(z_lo + 3, 4)
    z_far = lax.rem(z_lo + 2, 4)
    x_next, x_prev, x_far = lax.rem(x + 1, 4), lax.rem(x + 3, 4), lax.rem(x + 2, 4)

    def to(ref, k, i, peer):
        return remote(ref, ref, ws.at[k, i], wr.at[k, i], peer)

    sent = []

    def send(ref, k, i, peer):
        cp = to(ref, k, i, peer)
        cp.start()
        sent.append(cp)

    def arrived(ref, k, i):
        to(ref, k, i, sibling).wait_recv()

    def send_own(k):
        send(shard(k, z_lo), k, 0, up)
        send(shard(k, z_lo), k, 1, down)

    for k in range(AHEAD):
        send_own(k)

    def piece(i, h, row):
        is_self = jnp.logical_and(jnp.logical_and(c == z_hi, c == h), half == i)
        src, dst = feat.at[i, 3 * h + row], xbuf.at[own, row]
        there = device(x, 2 * i + parity, c * 4 + z_lo, jnp.int32(h))
        copy = remote(src, dst, fs.at[2 * i + h, row], fr.at[own, row], there)
        return is_self, copy, lambda: pltpu.make_async_copy(src, dst, fr.at[own, row]).start()

    def send_piece(i, h, row):
        is_self, copy, local = piece(i, h, row)

        @pl.when(is_self)
        def _():
            local()

        @pl.when(jnp.logical_not(is_self))
        def _():
            copy.start()

    pieces = [(i, h, row) for row in range(3) for i in range(2) for h in range(2)]

    col = lax.broadcasted_iota(jnp.int32, (64, 1024), 0)

    def features_arrive(arriving):
        first, count = arriving[0], len(arriving)
        for b in range(4):
            for row in arriving:
                pltpu.make_async_copy(xbuf.at[b, row], xbuf.at[b, row], fr.at[b, row]).wait()

        def body(b, part):
            for row in arriving:
                v = xbuf[b, row].astype(F32)
                xright[b, row] = jnp.where(col >= 4, pltpu.roll(v, 4, 0), 0.0).astype(BF16)
                xleft[b, row] = jnp.where(col < 60, pltpu.roll(v, 60, 0), 0.0).astype(BF16)
                part = part + v.reshape(8, 8, 1024).sum(axis=0)
            return part

        part = jnp.zeros((8, 1024), F32) if first == 0 else pool_buf[0]
        pool_buf[0] = lax.fori_loop(0, 4, body, part)
        if arriving[-1] == 2:
            for i, peer in enumerate(pool_peers):
                remote(pool_buf.at[0], pool_buf.at[i + 1], ps.at[i], pr.at[i], peer).start()
        acc[:, first : first + count, :, 0:256] = jnp.dot(
            xbuf[:, first : first + count].reshape(count * 256, 1024), point_w[...],
            preferred_element_type=F32,
        ).reshape(4, count, 64, 256)

    def compute(k, row, rows):
        branch, kh = ORDER[k]
        step = branch + 1
        n = 4 if kh == 1 else 4 - step
        src = (pl.ds((0, 0, step)[kh], n), pl.ds(row, rows))
        dst = (pl.ds((step, 0, 0)[kh], n), pl.ds(row, rows))
        lanes = pl.ds(256 * (branch + 1), 256)

        def times(lhs, kw):
            m = lhs.shape[2]
            w = wbuf[9 * branch + 3 * kh + kw].reshape(1024, 256)
            return jnp.dot(
                lhs.reshape(n * rows * m, 1024), w, preferred_element_type=F32
            ).reshape(n, rows, m, 256)

        mid = times(xbuf[src], 1)
        if kh == 1:
            acc[*dst, :, lanes] = mid
        else:
            acc[*dst, :, lanes] += mid
        if branch == 0:
            acc[*dst, 8:64, lanes] += times(xright[src], 0)[:, :, 0:56]
            acc[*dst, 0:56, lanes] += times(xleft[src], 2)[:, :, 8:64]
        elif branch == 1:
            acc[*dst, 24:64, lanes] += times(xbuf[*src, 0:48], 0)[:, :, 0:40]
            acc[*dst, 0:40, lanes] += times(xbuf[*src, 16:64], 2)[:, :, 8:48]
        else:
            acc[*dst, 32:64, lanes] += times(xright[*src, 0:32], 0)
            acc[*dst, 0:32, lanes] += times(xleft[*src, 32:64], 2)

    here = set()
    z_own, z_rest = 2 * parity, 2 - 2 * parity
    z_first, z_given, z_missing = parity, 3 * parity, 3 - 3 * parity
    for t in range(CHUNKS + 5):
        for k in (2 * t, 2 * t + 1):
            if k < CHUNKS:
                arrived(shard(k, z_prev), k, 0)
                send(shard(k, z_prev, 16), k, 2, up)
                arrived(shard(k, z_next), k, 1)
                send(shard(k, z_next, 0), k, 3, down)
            if k + AHEAD < CHUNKS:
                send_own(k + AHEAD)
        k = t - 1
        if 0 <= k < CHUNKS:
            arrived(shard(k, z_far, 16), k, 2)
            arrived(shard(k, z_far, 0), k, 3)
            send(column(k, x, c, z_first, 3), k, 4, right)
            send(column(k, x, c, z_first, 3), k, 5, left)
        done = sum(PER_STEP[:t])
        for p in pieces[done : done + sum(PER_STEP[t : t + 1])]:
            send_piece(*p)
        k = t - 2
        if 0 <= k < CHUNKS:
            arrived(column(k, x_prev, c, z_first, 3), k, 4)
            send(column(k, x_prev, c, z_own + 1, 1), k, 6, right)
            arrived(column(k, x_next, c, z_first, 3), k, 5)
            send(column(k, x_next, c, z_own, 1), k, 7, left)
            send(column(k, x_prev, c, z_given, 1), k, 11, y_up)
            send(column(k, x_next, c, z_given, 1), k, 12, y_down)
        k = t - 3
        if 0 <= k < CHUNKS:
            arrived(column(k, x_far, c, z_own + 1, 1), k, 6)
            arrived(column(k, x_far, c, z_own, 1), k, 7)
            send(column(k, x_far, c, z_own, 1), k, 9, y_up)
            send(column(k, x_far, c, z_own + 1, 1), k, 10, y_down)
        k = t - 4
        if 0 <= k < CHUNKS:
            arrived(column(k, x_far, c, z_rest, 1), k, 9)
            arrived(column(k, x_far, c, z_rest + 1, 1), k, 10)
            arrived(column(k, x_prev, c, z_missing, 1), k, 11)
            arrived(column(k, x_next, c, z_missing, 1), k, 12)
            send(whole(k, c), k, 8, sibling)
        arriving, work = WORK.get(t, ((), ()))
        if t == 6:
            for cp in dense:
                cp.wait()
        if arriving:
            features_arrive(arriving)
        for k, row, rows in work:
            if k not in here:
                here.add(k)
                arrived(whole(k, other), k, 8)
            compute(k, row, rows)

    for cp in sent:
        cp.wait_send()

    mine = group[image]
    spot = x * 2 + c

    def all_reduce(msg, got, red, sum_y, sum_z, full, s_sem, r_sem):
        def peer(o):
            s = lax.rem(spot + o, 8)
            return s, device(s // 2, y, z, lax.rem(s, 2))

        copies = []

        def go(src, dst, i, to_):
            cp = remote(src, dst, s_sem.at[i], r_sem.at[i], to_)
            cp.start()
            copies.append(cp)

        for o in range(1, 8):
            s, to_ = peer(o)
            go(msg.at[s], got.at[o - 1], o - 1, to_)
        total = msg[spot]
        for o in range(1, 8):
            copies[o - 1].wait_recv()
            total = total + got[o - 1]
        red[0] = total
        for o in range(1, 4):
            go(red.at[0], sum_y.at[o - 1], 6 + o, device(x, y + o, z, c))
        for o in range(1, 4):
            copies[6 + o].wait_recv()
            total = total + sum_y[o - 1]
        red[1] = total
        for o in range(1, 8):
            go(red.at[1], sum_z.at[o - 1], 9 + o, device(x, y, z + o, c))
        for o in range(1, 8):
            copies[9 + o].wait_recv()
            total = total + sum_z[o - 1]
        full[spot] = total
        for o in range(1, 8):
            s, to_ = peer(o)
            go(full.at[spot], full.at[spot], 16 + o, to_)
        for o in range(1, 8):
            s = lax.rem(spot - o + 8, 8)
            remote(full.at[s], full.at[s], s_sem.at[16 + o], r_sem.at[16 + o], sibling).wait_recv()
        return copies

    def add_up(t, carry):
        first, second = carry
        v = acc[t // 3, lax.rem(t, 3)].reshape(8, 8, 1024)
        return first + v.sum(axis=0), second + (v * v).sum(axis=0)

    zero = jnp.zeros((8, 1024), F32)
    first, second = lax.fori_loop(0, 12, add_up, (zero, zero))
    first = jnp.sum(first, axis=0, keepdims=True)
    second = jnp.sum(second, axis=0, keepdims=True)
    labels = lax.broadcasted_iota(jnp.int32, (16, 128), 0)
    for s in range(8):
        lanes = slice(128 * s, 128 * (s + 1))
        msg_a[s, 0:16] = jnp.where(labels == mine, first[:, lanes], 0.0)
        msg_a[s, 16:32] = jnp.where(labels == mine, second[:, lanes], 0.0)
    waits = all_reduce(msg_a, got_a, red_a, sum_y_a, sum_z_a, all_a, as_a, ar_a)

    means, invs = [], []
    for s in range(8):
        g1 = jnp.sum(jnp.where(labels == mine, all_a[s, 0:16], 0.0), axis=0, keepdims=True)
        g2 = jnp.sum(jnp.where(labels == mine, all_a[s, 16:32], 0.0), axis=0, keepdims=True)
        mean = g1 / COUNT
        means.append(mean)
        invs.append(lax.rsqrt(g2 / COUNT - mean * mean + 1e-05))
    mean = jnp.concatenate(means, axis=1)
    inv = jnp.concatenate(invs, axis=1)

    for i in range(3):
        remote(pool_buf.at[i + 1], pool_buf.at[i + 1], ps.at[i], pr.at[i], sibling).wait()
    pool = pool_buf[0] + pool_buf[1] + pool_buf[2] + pool_buf[3]
    pooled = (jnp.sum(pool, axis=0, keepdims=True) / PIXELS).astype(BF16)
    pooled = jnp.broadcast_to(pooled, (16, 1024))
    act = jnp.maximum(jnp.dot(pooled, pool_w[...], preferred_element_type=F32), 0.0).astype(BF16)
    pool_row = jnp.dot(act, proj_w[1024:1280], preferred_element_type=F32)[0:1]

    gains = jnp.concatenate([gain[i : i + 1] for i in range(4)], axis=1)
    shifts = jnp.concatenate([shift[i : i + 1] for i in range(4)], axis=1)

    def project(b, carry):
        first, second = carry
        v = acc[b].reshape(192, 1024)
        v = (v - mean) * inv * gains + shifts
        v = jnp.maximum(v, 0.0).astype(BF16)
        p = jnp.dot(v, proj_w[0:1024], preferred_element_type=F32) + pool_row
        proj[b] = p
        p = p.reshape(24, 8, 256)
        return first + p.sum(axis=0), second + (p * p).sum(axis=0)

    zero = jnp.zeros((8, 256), F32)
    first, second = lax.fori_loop(0, 4, project, (zero, zero))
    first = jnp.sum(first, axis=0, keepdims=True)
    second = jnp.sum(second, axis=0, keepdims=True)
    row = lax.broadcasted_iota(jnp.int32, (8, 128), 0)
    kind = lax.rem(row, 4)
    base = jnp.where(
        kind == 0, first[:, 0:128],
        jnp.where(kind == 1, first[:, 128:256], jnp.where(kind == 2, second[:, 0:128], second[:, 128:256])),
    )
    for s in range(8):
        msg_b[s] = jnp.where(2 * s + row // 4 == mine, base, 0.0)
    waits += all_reduce(msg_b, got_b, red_b, sum_y_b, sum_z_b, all_b, as_b, ar_b)
    total = jnp.zeros((8, 128), F32)
    for s in range(8):
        total = total + jnp.where(2 * s + row // 4 == mine, all_b[s], 0.0)

    def pick(i):
        return jnp.sum(jnp.where(kind == i, total, 0.0), axis=0, keepdims=True)

    mean = jnp.concatenate([pick(0), pick(1)], axis=1) / COUNT
    inv = lax.rsqrt(jnp.concatenate([pick(2), pick(3)], axis=1) / COUNT - mean * mean + 1e-05)

    def finish(b):
        v = (proj[b] - mean) * inv * pgain[...] + pshift[...]
        v = jnp.maximum(v, 0.0)
        for lane in range(2):
            halves[lane] = v[:, 128 * lane : 128 * (lane + 1)]
            for i in range(3):
                for k in range(2):
                    pair = halves[lane, pl.ds(64 * i + k, 32, stride=2), :]
                    tiles[lane, pl.ds(2 * i + k, 32, stride=8), :] = pair
        both = jnp.concatenate([tiles[0].reshape(32, 8, 128), tiles[1].reshape(32, 8, 128)], axis=1)
        sendbuf[pl.ds(32 * b, 32)] = both.astype(BF16)


    slot = image * 2 + c

    def scatter(e, b):
        e = lax.rem(d + e, 32)
        remote(
            sendbuf.at[32 * b + e], out.at[slot], end_send, end_recv, (e, 2 * b + parity)
        ).start()
        return b

    for turn in range(4):
        b = lax.rem(own + turn, 4)
        finish(b)
        if turn == 0:
            pltpu.make_async_copy(sendbuf.at[32 * own + d], out.at[slot], end_recv).start()
        lax.fori_loop(1 if turn == 0 else 0, 32, scatter, b)
    for cp in waits:
        cp.wait_send()
    for p in pieces:
        is_self, copy, _ = piece(*p)

        @pl.when(jnp.logical_not(is_self))
        def _():
            copy.wait_send()

    rest = sendbuf.at[pl.ds(0, 127)]
    pltpu.make_async_copy(rest, rest, end_send).wait()
    pltpu.make_async_copy(out, out, end_recv).wait()


def shards(
    features, first_w, second_w, third_w, point_w, pool_w, proj_w, gain, shift, pgain, pshift, group
):
    any_ = pl.BlockSpec(memory_space=pl.ANY)
    vmem = pl.BlockSpec(memory_space=pltpu.VMEM)
    smem = pl.BlockSpec(memory_space=pltpu.SMEM)
    dma = pltpu.SemaphoreType.DMA
    reduce_bufs = [
        pltpu.VMEM((n, rows, 128), F32) for rows in (32, 8) for n in (8, 7, 2, 3, 7, 8)
    ]
    out = pl.pallas_call(
        kernel,
        out_shape=jax.ShapeDtypeStruct((128, 16, 128), BF16),
        in_specs=[any_] * 7 + [vmem] * 4 + [smem],
        out_specs=any_,
        scratch_shapes=[
            pltpu.VMEM((27, 4, 4, 2, 32, 256), BF16),
            pltpu.VMEM((1024, 256), BF16),
            pltpu.VMEM((1024, 256), BF16),
            pltpu.VMEM((1280, 256), BF16),
            pltpu.VMEM((4, 3, 64, 1024), BF16),
            pltpu.VMEM((4, 3, 64, 1024), BF16),
            pltpu.VMEM((4, 3, 64, 1024), BF16),
            pltpu.VMEM((4, 3, 64, 1024), F32),
            pltpu.VMEM((4, 192, 256), F32),
            pltpu.VMEM((2, 192, 128), F32),
            pltpu.VMEM((2, 256, 128), F32),
            pltpu.VMEM((128, 16, 128), BF16),
            pltpu.VMEM((4, 8, 1024), F32),
            *reduce_bufs,
            dma((6,)), dma((CHUNKS, 13)), dma((CHUNKS, 13)), dma((4, 3)), dma((4, 3)), dma((3,)), dma((3,)),
            dma((24,)), dma((24,)), dma((24,)), dma((24,)), dma(()), dma(()),
        ],
        compiler_params=pltpu.CompilerParams(
            collective_id=0, has_side_effects=True, vmem_limit_bytes=56 << 20
        ),
        cost_estimate=pl.CostEstimate(flops=8_000_000_000, bytes_accessed=20_000_000, transcendentals=0),
    )(
        features, first_w.reshape(9, 32, 256), second_w.reshape(9, 32, 256), third_w.reshape(9, 32, 256),
        point_w, pool_w, proj_w, gain, shift,
        pgain.reshape(1, -1), pshift.reshape(1, -1), group,
    )
    out = out.reshape(64, 2, 2, 8, 128)[:, :, :, :6].reshape(64, 2, 2, 3, 2, 128)
    return out.transpose(0, 1, 3, 4, 2, 5).reshape(64, 6, 2, 256)


def solution(mesh):
    weight = P(None, None, "dp", None)
    in_specs = (P("dp", "rows", None, None), weight, weight, weight) + (P(),) * 8
    return jax.shard_map(
        shards, mesh=mesh, in_specs=in_specs, out_specs=P(None, "rows", "dp", None), check_vma=False
    )
```
